32 devices in a mesh: groups: 2 (over y), mp: 4 (over z), dp: 2 (over x), sub: 2 (over core).
Axes of the slice: x: 2, y: 2, z: 4, core: 2. Of those that a mesh axis runs over, the one named last changes fastest.
Arguments:
- gate_act: bfloat16 [5888, 512], P(('mp', 'dp', 'sub'), 'groups'), parts along dimension 1, may hold values from -6 to 6
- up_act: bfloat16 [5888, 512], P(('mp', 'dp', 'sub'), 'groups'), parts along dimension 1, may hold values from -6 to 6
- down_weight: bfloat16 [5888, 16384], P(('mp', 'dp', 'sub')), may hold values from -0.109375 to 0.109375
Outputs:
- mixed: bfloat16 [512, 4, 4096], P('groups', None, ('dp', 'sub')), parts along dimension 0
The draws below stay inside these ranges and needn't reach their ends.
There are 2 independent parts, one for each index of `groups`. The reference program is written for one: setup_inputs(seed, part) draws one part's arguments, and reference() takes and returns one part's arrays. A program takes and returns all parts, laid end to end along the dimension named above; an argument that names none is the same for every part. Nothing has to cross between parts.
All inputs are finite; a program needn't handle non-finite values.
Results may differ from the reference program's by a relative error of at most 0.014.
Values may be sent and summed in bfloat16 or wider, within the bound.
A program may use at most 64 MiB of HBM per device.

```python
import jax
import jax.numpy as jnp
from jax import lax

D = 16384
FF_DEV = 368
ROWS = 256
FF = 5888
N_MP = 4
N_DP = 2
N_SUB = 2


def spiked(entries, rng, source, target, shards_of, factor):
    def block_of(dim):
        return (jnp.arange(entries.shape[dim]) // (entries.shape[dim] // shards_of)).reshape((-1,) + (1,) * (entries.ndim - 1 - dim))

    one_side = jax.random.permutation(rng, shards_of)[block_of(target)]
    other_side = (block_of(target) + shards_of // 2) % shards_of
    return jnp.where((block_of(source) == one_side) | (block_of(source) == other_side), factor * entries, entries)


def levels(stream_key, extent, split, low, largest):
    gain, own = 1.0, jax.random.fold_in(stream_key, 6)
    for axis_at, parts in split:
        draws = jnp.exp(jax.random.uniform(jax.random.fold_in(own, axis_at), (parts,), jnp.float32, low / len(split), largest / len(split)))
        gain = gain * jnp.repeat(draws, extent[axis_at] // parts).reshape([-1 if axis == axis_at else 1 for axis in range(len(extent))])
    return gain


def noise(rng, dims, scale, most, pieces=(), held_as=jnp.bfloat16):
    entries = scale * jax.random.normal(rng, dims, jnp.float32)
    if pieces:
        entries = entries * levels(rng, dims, pieces, -0.22, 0.18)
    return jnp.clip(entries, -most, most).astype(held_as)


def noise_with(stream_key, shape, spread, limit, cuts, heavy, kind=jnp.bfloat16):
    drawn = spread * jax.random.normal(stream_key, shape, jnp.float32)
    if cuts:
        drawn = drawn * levels(stream_key, shape, cuts, -0.22, 0.18)
    return jnp.clip(spiked(drawn, jax.random.fold_in(stream_key, 3), *heavy), -limit, limit).astype(kind)


def setup_inputs(seed: int = 0, part: int = 0) -> dict:
    seeds = jax.random.split(jax.random.key(seed), 4)
    own_keys = jax.random.split(jax.random.fold_in(seeds[3], part), 4)
    return {
        "gate_act": noise(own_keys[0], (FF, ROWS), 1.0, 6.0, ((0, 16),)),
        "up_act": noise(own_keys[1], (FF, ROWS), 1.0, 6.0, ((0, 16),)),
        "down_weight": noise_with(seeds[2], (FF, D), FF ** -0.5, 0.109375, ((0, 16),), (0, 1, 16, 2.0)),
    }


def reference(gate_act, up_act, down_weight):
    hidden = (jax.nn.silu(gate_act.astype(jnp.float32)) * up_act.astype(jnp.float32)).astype(jnp.bfloat16)
    segs = N_DP * N_SUB
    hidden_blocks = hidden.reshape(N_MP, segs, FF_DEV, ROWS)
    weight_blocks = down_weight.reshape(N_MP, segs, FF_DEV, D)

    def segment_sum(total, k):
        def add_term(acc, m):
            term = lax.dot_general(hidden_blocks[m, k], weight_blocks[m, k], (((0,), (0,)), ((), ())), preferred_element_type=jnp.float32)
            rounded = lax.optimization_barrier(term.astype(jnp.bfloat16))
            return acc + rounded.astype(jnp.float32), None

        acc, unused = lax.scan(add_term, jnp.zeros((ROWS, D), jnp.float32), jnp.arange(N_MP, dtype=jnp.int32))
        partial_sum = lax.optimization_barrier(acc.astype(jnp.bfloat16))
        return total + partial_sum.astype(jnp.float32), None

    total, unused = lax.scan(segment_sum, jnp.zeros((ROWS, D), jnp.float32), jnp.arange(segs, dtype=jnp.int32))
    return total.astype(jnp.bfloat16).reshape(ROWS, N_MP, D // N_MP)
```

```python
import functools

import jax
import jax.numpy as jnp
from jax import lax
from jax.experimental import pallas as pl
from jax.experimental.pallas import tpu as pltpu
from jax.sharding import PartitionSpec as P

MESH = pl.DeviceIdType.MESH
F32, BF16 = jnp.float32, jnp.bfloat16

WIDE, TALL = 256, 128
LAG_SUB, LAG_DP, LAG_MP = 2, 2, 2


def kernel(
    sizes, gate, up, weight, out, hidden, held, sub_tx, sub_rx, dp_tx, dp_rx, mp_tx, mp_rx,
    w_sem, sub_send, sub_recv, dp_send, dp_recv, mp_send, mp_recv,
):
    n_mp, n_dp, n_sub = sizes
    depth, rows = gate.shape
    width = out.shape[2]
    wide, tall = mp_tx.shape[2], mp_tx.shape[1]
    per_j, per_c = width // wide, rows // tall
    messages = mp_tx.shape[0]
    z, x, s = lax.axis_index("mp"), lax.axis_index("dp"), lax.axis_index("sub")
    owner = n_mp // 2
    below, above = z < owner, z > owner

    barrier = pltpu.get_barrier_semaphore()
    for i in range(1, n_sub):
        pl.semaphore_signal(barrier, inc=1, device_id={"sub": lax.rem(s + i, n_sub)}, device_id_type=MESH)
    for i in range(1, n_dp):
        pl.semaphore_signal(barrier, inc=1, device_id={"dp": lax.rem(x + i, n_dp)}, device_id_type=MESH)

    @pl.when(z > 0)
    def _():
        pl.semaphore_signal(barrier, inc=1, device_id={"mp": z - 1}, device_id_type=MESH)

    @pl.when(z < n_mp - 1)
    def _():
        pl.semaphore_signal(barrier, inc=1, device_id={"mp": z + 1}, device_id_type=MESH)

    def load(j):
        span = weight.shape[1] // n_mp
        return pltpu.make_async_copy(
            weight.at[:, pl.ds(pl.multiple_of(j * span, 128), span)], held.at[j, pl.ds(0, depth)], w_sem.at[j]
        )

    for j in range(n_mp):
        load(j).start()

    pad = hidden.shape[1] - depth
    if pad:
        for j in range(n_mp):
            held[j, depth:, :] = jnp.zeros((pad, held.shape[2]), BF16)
    for side in range(2):
        mp_rx[side, messages] = jnp.zeros((tall, wide), BF16)
    g, u = gate[...].astype(F32), up[...].astype(F32)
    h = g / (1.0 + jnp.exp(-g)) * u
    if pad:
        h = jnp.concatenate([h, jnp.zeros((pad, rows), F32)], axis=0)
    hidden[...] = jnp.transpose(h).astype(BF16)

    neighbours = jnp.where(z > 0, 1, 0) + jnp.where(z < n_mp - 1, 1, 0)
    pl.semaphore_wait(barrier, n_sub - 1 + n_dp - 1 + neighbours)

    def place(m):
        c, r = m // per_c, m % per_c
        return c // per_j, pl.multiple_of((c % per_j) * wide, 128), pl.multiple_of(r * tall, tall)

    def result(m):
        j, col, row = place(m)
        return out.at[j, pl.ds(row, tall), pl.ds(col, wide)]

    def term(m, d, k):
        j, col, row = place(m)
        first = pl.multiple_of((d * n_sub + k) * width + col, 128)
        return jnp.dot(
            hidden[pl.ds(row, tall), :], held[j, :, pl.ds(first, wide)], preferred_element_type=F32
        )

    def sub_copy(m, i):
        return pltpu.make_async_remote_copy(
            src_ref=sub_tx.at[m, i - 1],
            dst_ref=sub_rx.at[m, n_sub - i - 1],
            send_sem=sub_send.at[i - 1],
            recv_sem=sub_recv.at[m, n_sub - i - 1],
            device_id={"sub": lax.rem(s + i, n_sub)},
            device_id_type=MESH,
        )

    def dp_copy(m, i):
        return pltpu.make_async_remote_copy(
            src_ref=dp_tx.at[m, i - 1],
            dst_ref=dp_rx.at[m, n_dp - i - 1],
            send_sem=dp_send.at[i - 1],
            recv_sem=dp_recv.at[m, n_dp - i - 1],
            device_id={"dp": lax.rem(x + i, n_dp)},
            device_id_type=MESH,
        )

    def mp_copy(src, dst, m, side):
        return pltpu.make_async_remote_copy(
            src_ref=src,
            dst_ref=dst,
            send_sem=mp_send.at[side],
            recv_sem=mp_recv.at[1 - side, m],
            device_id={"mp": z - 1 if side == 0 else z + 1},
            device_id_type=MESH,
        )

    def arrived(ref, sem):
        pltpu.make_async_copy(ref, ref, sem).wait()

    def to_core(m):
        j = m // (per_c * per_j)

        @pl.when(m % (per_c * per_j) == 0)
        def _():
            load(j).wait()

        for i in range(1, n_sub):
            for d in range(n_dp):
                sub_tx[m, i - 1, d] = term(m, d, lax.rem(s + i, n_sub)).astype(BF16)
            sub_copy(m, i).start()

    def to_dp(m):
        for i in range(1, n_sub):
            arrived(sub_rx.at[m, i - 1], sub_recv.at[m, i - 1])
        for i in range(1, n_dp):
            d = lax.rem(x + i, n_dp)
            total = term(m, d, s)
            for k in range(1, n_sub):
                total += sub_rx[m, k - 1, d].astype(F32)
            dp_tx[m, i - 1] = total.astype(BF16)
            dp_copy(m, i).start()

    from_low = (z > 0) & (z <= owner)
    from_high = (z < n_mp - 1) & (z >= owner)

    def to_owner(m):
        total = term(m, x, s)
        for k in range(1, n_sub):
            total += sub_rx[m, k - 1, x].astype(F32)
        for i in range(1, n_dp):
            arrived(dp_rx.at[m, i - 1], dp_recv.at[m, i - 1])
        for i in range(1, n_dp):
            total += dp_rx[m, i - 1].astype(F32)

        @pl.when(from_low)
        def _():
            arrived(mp_rx.at[0, m], mp_recv.at[0, m])

        @pl.when(from_high)
        def _():
            arrived(mp_rx.at[1, m], mp_recv.at[1, m])

        total += mp_rx[0, jnp.where(from_low, m, messages)].astype(F32)
        total += mp_rx[1, jnp.where(from_high, m, messages)].astype(F32)
        summed = total.astype(BF16)

        @pl.when(z == owner)
        def _():
            j, col, row = place(m)
            out[j, pl.ds(row, tall), pl.ds(col, wide)] = summed
            if owner > 0:
                mp_copy(result(m), result(m), m, 0).start()
            if owner < n_mp - 1:
                mp_copy(result(m), result(m), m, 1).start()

        @pl.when(z != owner)
        def _():
            mp_tx[m] = summed

        @pl.when(below)
        def _():
            mp_copy(mp_tx.at[m], mp_rx.at[0, m], m, 1).start()

        @pl.when(above)
        def _():
            mp_copy(mp_tx.at[m], mp_rx.at[1, m], m, 0).start()

    def from_owner(m):
        @pl.when(below)
        def _():
            arrived(result(m), mp_recv.at[1, m])

        @pl.when(above)
        def _():
            arrived(result(m), mp_recv.at[0, m])

        @pl.when(below & (z > 0))
        def _():
            mp_copy(result(m), result(m), m, 0).start()

        @pl.when(above & (z < n_mp - 1))
        def _():
            mp_copy(result(m), result(m), m, 1).start()

    far = max(owner, n_mp - 1 - owner)
    depth_in = jnp.where(z == owner, far, jnp.where(below, z, n_mp - 1 - z))
    depth_out = far + jnp.where(below, owner - z, z - owner)
    lag_in = LAG_SUB + LAG_DP + LAG_MP * depth_in
    lag_out = LAG_SUB + LAG_DP + LAG_MP * depth_out

    def stage(m, work):
        @pl.when((m >= 0) & (m < messages))
        def _():
            work(m)

    def step(t, carry):
        stage(t, to_core)
        stage(t - LAG_SUB, to_dp)
        stage(t - lag_in, to_owner)
        stage(t - lag_out, from_owner)
        return carry

    lax.fori_loop(0, messages + LAG_SUB + LAG_DP + LAG_MP * 2 * far, step, 0)

    for i in range(1, n_sub):
        arrived(sub_tx.at[:, i - 1], sub_send.at[i - 1])
    for i in range(1, n_dp):
        arrived(dp_tx.at[:, i - 1], dp_send.at[i - 1])

    @pl.when(z > 0)
    def _():
        arrived(mp_tx, mp_send.at[0])

    @pl.when(z < n_mp - 1)
    def _():
        arrived(mp_tx, mp_send.at[1])


def solution(mesh):
    n_mp, n_dp, n_sub = (mesh.shape[axis] for axis in ("mp", "dp", "sub"))

    def shards(gate, up, weight):
        depth, rows = gate.shape
        features = weight.shape[1]
        width = features // (n_mp * n_dp * n_sub)
        wide, tall = min(WIDE, width), min(TALL, rows)
        messages = n_mp * (width // wide) * (rows // tall)
        padded = -(-depth // 128) * 128
        parts = pl.pallas_call(
            functools.partial(kernel, (n_mp, n_dp, n_sub)),
            out_shape=jax.ShapeDtypeStruct((n_mp, rows, width), BF16),
            in_specs=[
                pl.BlockSpec(memory_space=pltpu.VMEM),
                pl.BlockSpec(memory_space=pltpu.VMEM),
                pl.BlockSpec(memory_space=pl.ANY),
            ],
            out_specs=pl.BlockSpec(memory_space=pltpu.VMEM),
            scratch_shapes=[
                pltpu.VMEM((rows, padded), BF16),
                pltpu.VMEM((n_mp, padded, features // n_mp), BF16),
                pltpu.VMEM((messages, n_sub - 1, n_dp, tall, wide), BF16),
                pltpu.VMEM((messages, n_sub - 1, n_dp, tall, wide), BF16),
                pltpu.VMEM((messages, n_dp - 1, tall, wide), BF16),
                pltpu.VMEM((messages, n_dp - 1, tall, wide), BF16),
                pltpu.VMEM((messages, tall, wide), BF16),
                pltpu.VMEM((2, messages + 1, tall, wide), BF16),
                pltpu.SemaphoreType.DMA((n_mp,)),
                pltpu.SemaphoreType.DMA((n_sub - 1,)),
                pltpu.SemaphoreType.DMA((messages, n_sub - 1)),
                pltpu.SemaphoreType.DMA((n_dp - 1,)),
                pltpu.SemaphoreType.DMA((messages, n_dp - 1)),
                pltpu.SemaphoreType.DMA((2,)),
                pltpu.SemaphoreType.DMA((2, messages)),
            ],
            compiler_params=pltpu.CompilerParams(
                collective_id=0, has_side_effects=True, vmem_limit_bytes=56 * 1024 * 1024
            ),
            cost_estimate=pl.CostEstimate(
                flops=2 * rows * depth * features,
                bytes_accessed=2 * depth * features,
                transcendentals=rows * depth,
            ),
            name="down_sum",
        )(gate, up, weight)
        return jnp.transpose(parts, (1, 0, 2))

    placed = (
        P(("mp", "dp", "sub"), "groups"),
        P(("mp", "dp", "sub"), "groups"),
        P(("mp", "dp", "sub"), None),
    )
    return jax.shard_map(
        shards,
        mesh=mesh,
        in_specs=placed,
        out_specs=P("groups", None, ("dp", "sub")),
        check_vma=False,
    )
```

```python
import functools

import jax
import jax.numpy as jnp
from jax import lax
from jax.experimental import pallas as pl
from jax.experimental.pallas import tpu as pltpu
from jax.sharding import PartitionSpec as P

MESH = pl.DeviceIdType.MESH
F32, BF16 = jnp.float32, jnp.bfloat16

WIDE, TALL = 256, 64
LAG_DP, LAG_MP = 5, 5


def kernel(
    sizes, gate, up, weight, out, hidden, held, sub_tx, sub_rx, dp_tx, dp_rx, own, mp_tx, mp_rx, done,
    w_sem, sub_send, sub_recv, dp_send, dp_recv, mp_send, mp_recv,
):
    n_mp, n_dp, n_sub = sizes
    depth, rows = gate.shape
    width = out.shape[2]
    messages, tall, wide = mp_tx.shape
    chunks = held.shape[0]
    per_c = rows // tall
    z, x, s = lax.axis_index("mp"), lax.axis_index("dp"), lax.axis_index("sub")
    owner = n_mp // 2
    below, above = z < owner, z > owner

    barrier = pltpu.get_barrier_semaphore()
    for i in range(1, n_sub):
        pl.semaphore_signal(barrier, inc=1, device_id={"sub": lax.rem(s + i, n_sub)}, device_id_type=MESH)
    for i in range(1, n_dp):
        pl.semaphore_signal(barrier, inc=1, device_id={"dp": lax.rem(x + i, n_dp)}, device_id_type=MESH)

    @pl.when(z > 0)
    def _():
        pl.semaphore_signal(barrier, inc=1, device_id={"mp": z - 1}, device_id_type=MESH)

    @pl.when(z < n_mp - 1)
    def _():
        pl.semaphore_signal(barrier, inc=1, device_id={"mp": z + 1}, device_id_type=MESH)

    def load(c):
        for q in range(n_dp * n_sub):
            first = ((c % n_mp) * n_dp * n_sub + q) * width + (c // n_mp) * wide
            pltpu.make_async_copy(
                weight.at[:, pl.ds(pl.multiple_of(first, 128), wide)],
                held.at[c, pl.ds(0, depth), pl.ds(q * wide, wide)],
                w_sem.at[c],
            ).start()

    lax.fori_loop(0, chunks, lambda c, carry: (load(c), carry)[1], 0)

    pad = hidden.shape[1] - depth
    if pad:
        for c in range(chunks):
            held[c, depth:, :] = jnp.zeros((pad, held.shape[2]), BF16)
    for side in range(2):
        mp_rx[side, messages] = jnp.zeros((tall, wide), BF16)
    g, u = gate[...].astype(F32), up[...].astype(F32)
    h = g / (1.0 + jnp.exp(-g)) * u
    if pad:
        h = jnp.concatenate([h, jnp.zeros((pad, rows), F32)], axis=0)
    hidden[...] = jnp.transpose(h).astype(BF16)

    neighbours = jnp.where(z > 0, 1, 0) + jnp.where(z < n_mp - 1, 1, 0)
    pl.semaphore_wait(barrier, n_sub - 1 + n_dp - 1 + neighbours)

    def term(c, d, k):
        first = pl.multiple_of((d * n_sub + k) * wide, 128)
        return jnp.dot(hidden[...], held[c, :, pl.ds(first, wide)], preferred_element_type=F32)

    def sub_copy(c, i):
        return pltpu.make_async_remote_copy(
            src_ref=sub_tx.at[c, i - 1],
            dst_ref=sub_rx.at[c, n_sub - i - 1],
            send_sem=sub_send.at[i - 1],
            recv_sem=sub_recv.at[c, n_sub - i - 1],
            device_id={"sub": lax.rem(s + i, n_sub)},
            device_id_type=MESH,
        )

    def dp_copy(m, i):
        return pltpu.make_async_remote_copy(
            src_ref=dp_tx.at[i - 1, m],
            dst_ref=dp_rx.at[n_dp - i - 1, m],
            send_sem=dp_send.at[i - 1],
            recv_sem=dp_recv.at[n_dp - i - 1, m],
            device_id={"dp": lax.rem(x + i, n_dp)},
            device_id_type=MESH,
        )

    def mp_copy(src, dst, m, side):
        return pltpu.make_async_remote_copy(
            src_ref=src,
            dst_ref=dst,
            send_sem=mp_send.at[side],
            recv_sem=mp_recv.at[1 - side, m],
            device_id={"mp": z - 1 if side == 0 else z + 1},
            device_id_type=MESH,
        )

    def arrived(ref, sem):
        pltpu.make_async_copy(ref, ref, sem).wait()

    def to_core(c):
        arrived(held.at[c, pl.ds(0, depth)], w_sem.at[c])
        for i in range(1, n_sub):
            for d in range(n_dp):
                sub_tx[c, i - 1, d] = term(c, d, lax.rem(s + i, n_sub)).astype(BF16)
            sub_copy(c, i).start()

    def chip_term(c, d):
        total = term(c, d, s)
        for k in range(1, n_sub):
            total += sub_rx[c, k - 1, d].astype(F32)
        return total

    def to_dp(c):
        for i in range(1, n_sub):
            arrived(sub_rx.at[c, i - 1], sub_recv.at[c, i - 1])
        for i in range(1, n_dp):
            total = chip_term(c, lax.rem(x + i, n_dp)).astype(BF16)
            for r in range(per_c):
                dp_tx[i - 1, c * per_c + r] = total[r * tall : (r + 1) * tall]
                dp_copy(c * per_c + r, i).start()

    def keep(c):
        total = chip_term(c, x)
        for r in range(per_c):
            own[c * per_c + r] = total[r * tall : (r + 1) * tall]

    from_low = (z > 0) & (z <= owner)
    from_high = (z < n_mp - 1) & (z >= owner)

    def to_owner(m):
        for i in range(1, n_dp):
            arrived(dp_rx.at[i - 1, m], dp_recv.at[i - 1, m])

        @pl.when(from_low)
        def _():
            arrived(mp_rx.at[0, m], mp_recv.at[0, m])

        @pl.when(from_high)
        def _():
            arrived(mp_rx.at[1, m], mp_recv.at[1, m])

        total = own[m]
        for i in range(1, n_dp):
            total += dp_rx[i - 1, m].astype(F32)
        total += mp_rx[0, jnp.where(from_low, m, messages)].astype(F32)
        total += mp_rx[1, jnp.where(from_high, m, messages)].astype(F32)
        summed = total.astype(BF16)

        @pl.when(z == owner)
        def _():
            done[m] = summed
            if owner > 0:
                mp_copy(done.at[m], done.at[m], m, 0).start()
            if owner < n_mp - 1:
                mp_copy(done.at[m], done.at[m], m, 1).start()
            write(m)

        @pl.when(z != owner)
        def _():
            mp_tx[m] = summed

        @pl.when(below)
        def _():
            mp_copy(mp_tx.at[m], mp_rx.at[0, m], m, 1).start()

        @pl.when(above)
        def _():
            mp_copy(mp_tx.at[m], mp_rx.at[1, m], m, 0).start()

    def write(m):
        c, r = m // per_c, m % per_c

        @pl.when(c % n_mp == n_mp - 1)
        def _():
            blocks = [done[m - (n_mp - 1 - j) * per_c].astype(F32) for j in range(n_mp)]
            col = pl.multiple_of((c // n_mp) * wide, 128)
            out[pl.ds(r * tall, tall), :, pl.ds(col, wide)] = jnp.stack(blocks, axis=1).astype(BF16)

    def from_owner(m):
        @pl.when(below)
        def _():
            arrived(done.at[m], mp_recv.at[1, m])

        @pl.when(above)
        def _():
            arrived(done.at[m], mp_recv.at[0, m])

        @pl.when(below & (z > 0))
        def _():
            mp_copy(done.at[m], done.at[m], m, 0).start()

        @pl.when(above & (z < n_mp - 1))
        def _():
            mp_copy(done.at[m], done.at[m], m, 1).start()

        @pl.when(z != owner)
        def _():
            write(m)

    far = max(owner, n_mp - 1 - owner)
    depth_in = jnp.where(z == owner, far, jnp.where(below, z, n_mp - 1 - z))
    depth_out = far + jnp.where(below, owner - z, z - owner)
    lag_in = per_c + LAG_DP + LAG_MP * depth_in
    lag_out = per_c + LAG_DP + LAG_MP * depth_out

    def stage(m, count, work):
        @pl.when((m >= 0) & (m < count))
        def _():
            work(m)

    def step(k, carry):
        for r in range(per_c):
            if r == 0:
                stage(k, chunks, to_core)
            if r == min(1, per_c - 1):
                stage(k - 1, chunks, to_dp)
            if r == min(2, per_c - 1):
                stage(k - 1, chunks, keep)
            stage(k * per_c + r - lag_in, messages, to_owner)
            stage(k * per_c + r - lag_out, messages, from_owner)
        return carry

    last = messages + per_c + LAG_DP + LAG_MP * 2 * far
    lax.fori_loop(0, -(-last // per_c), step, 0)

    for i in range(1, n_sub):
        arrived(sub_tx.at[:, i - 1], sub_send.at[i - 1])
    for i in range(1, n_dp):
        arrived(dp_tx.at[i - 1], dp_send.at[i - 1])

    @pl.when(z > 0)
    def _():
        arrived(mp_tx, mp_send.at[0])

    @pl.when(z < n_mp - 1)
    def _():
        arrived(mp_tx, mp_send.at[1])


def solution(mesh):
    n_mp, n_dp, n_sub = (mesh.shape[axis] for axis in ("mp", "dp", "sub"))

    def shards(gate, up, weight):
        depth, rows = gate.shape
        features = weight.shape[1]
        width = features // (n_mp * n_dp * n_sub)
        wide, tall = min(WIDE, width), min(TALL, rows)
        chunks = n_mp * (width // wide)
        messages = chunks * (rows // tall)
        padded = -(-depth // 128) * 128
        return pl.pallas_call(
            functools.partial(kernel, (n_mp, n_dp, n_sub)),
            out_shape=jax.ShapeDtypeStruct((rows, n_mp, width), BF16),
            in_specs=[
                pl.BlockSpec(memory_space=pltpu.VMEM),
                pl.BlockSpec(memory_space=pltpu.VMEM),
                pl.BlockSpec(memory_space=pl.ANY),
            ],
            out_specs=pl.BlockSpec(memory_space=pltpu.VMEM),
            scratch_shapes=[
                pltpu.VMEM((rows, padded), BF16),
                pltpu.VMEM((chunks, padded, n_dp * n_sub * wide), BF16),
                pltpu.VMEM((chunks, n_sub - 1, n_dp, rows, wide), BF16),
                pltpu.VMEM((chunks, n_sub - 1, n_dp, rows, wide), BF16),
                pltpu.VMEM((n_dp - 1, messages, tall, wide), BF16),
                pltpu.VMEM((n_dp - 1, messages, tall, wide), BF16),
                pltpu.VMEM((messages, tall, wide), F32),
                pltpu.VMEM((messages, tall, wide), BF16),
                pltpu.VMEM((2, messages + 1, tall, wide), BF16),
                pltpu.VMEM((messages, tall, wide), BF16),
                pltpu.SemaphoreType.DMA((chunks,)),
                pltpu.SemaphoreType.DMA((n_sub - 1,)),
                pltpu.SemaphoreType.DMA((chunks, n_sub - 1)),
                pltpu.SemaphoreType.DMA((n_dp - 1,)),
                pltpu.SemaphoreType.DMA((n_dp - 1, messages)),
                pltpu.SemaphoreType.DMA((2,)),
                pltpu.SemaphoreType.DMA((2, messages)),
            ],
            compiler_params=pltpu.CompilerParams(
                collective_id=0, has_side_effects=True, vmem_limit_bytes=56 * 1024 * 1024
            ),
            cost_estimate=pl.CostEstimate(
                flops=2 * rows * depth * features,
                bytes_accessed=2 * depth * features,
                transcendentals=rows * depth,
            ),
            name="down_sum",
        )(gate, up, weight)

    placed = (
        P(("mp", "dp", "sub"), "groups"),
        P(("mp", "dp", "sub"), "groups"),
        P(("mp", "dp", "sub"), None),
    )
    return jax.shard_map(
        shards,
        mesh=mesh,
        in_specs=placed,
        out_specs=P("groups", None, ("dp", "sub")),
        check_vma=False,
    )
```
